512 devices in a mesh: sec: 64 (over y, z), yb: 8 (over x, core).
Axes of the slice: x: 4, y: 4, z: 16, core: 2. Of those that a mesh axis runs over, the one named last changes fastest.
Arguments:
- volume: float32 [64, 2048, 2048], P('sec', None, 'yb'), may hold values from 0 to 1
- block_ids: int32 [64, 8, 64], P('sec', 'yb'), may hold values from 0 to 127, as said below
- counts: int32 [64, 8], P('sec', 'yb'), may hold values from 1 to 64, as said below
Outputs:
- downsampled: float32 [32, 1024, 1024], P(None, 'sec', 'yb')
- coeffs: float32 [64, 8, 64, 512], P('sec', 'yb')
The draws below stay inside these ranges and needn't reach their ends.
Inputs may be any that keep to these rules, and one draw needn't show every extreme that they name: `block_ids`: each device's first counts entries are distinct block numbers; entries at later slots are 0. `counts`: some device has all 64 slots valid.
All inputs are finite; a program needn't handle non-finite values.
Results may differ from the reference program's by a relative error of at most 0.0003.
Values sent between devices are 32-bit elements; how exact they have to be, the bound alone decides.
A program may use at most 64 MiB of HBM per device.

```python
import math
import jax
import jax.numpy as jnp
from jax import lax

GROUP = 64
ROWS = 256
COLS_DEV = 32
COLUMNS = 2048
YROWS = 2048
NBLK = 128
SLOTS = 64
N_SEC = 64
N_YB = 8


def permute_one(subkey):
    return jax.random.permutation(subkey, NBLK)


def draw_shared(key):
    total = N_SEC * N_YB
    key_count, key_top, key_perm = jax.random.split(key, 3)
    counts = jax.random.randint(key_count, (total,), 1, SLOTS + 1)
    busiest = jax.random.randint(key_top, (), 0, total)
    counts = jnp.where(jnp.arange(total) == busiest, SLOTS, counts)
    orders = jax.vmap(permute_one)(jax.random.split(key_perm, total))[:, :SLOTS]
    block_ids = jnp.where(jnp.arange(SLOTS)[None, :] < counts[:, None], orders, 0)
    return (block_ids.reshape(N_SEC, N_YB, SLOTS).astype(jnp.int32), counts.reshape(N_SEC, N_YB).astype(jnp.int32))


def draw_block_ids(key, part):
    shared = draw_shared(key)
    return shared[0]


def draw_counts(key, part):
    shared = draw_shared(key)
    return shared[1]


def level_of(key, shape, cuts, least, top_value):
    gain, own = 1.0, jax.random.fold_in(key, 6)
    for position, shards_of in cuts:
        heights = jnp.exp(jax.random.uniform(jax.random.fold_in(own, position), (shards_of,), jnp.float32, least / len(cuts), top_value / len(cuts)))
        gain = gain * jnp.repeat(heights, shape[position] // shards_of).reshape([-1 if axis == position else 1 for axis in range(len(shape))])
    return gain


def setup_inputs(seed: int = 0) -> dict:
    keys = jax.random.split(jax.random.key(seed), 4)
    return {
        "volume": jnp.clip(1.0 * jax.random.uniform(keys[0], (GROUP, COLUMNS, YROWS), jnp.float32) ** level_of(keys[0], (GROUP, COLUMNS, YROWS), ((0, 64), (2, 8)), -0.2, 0.2), 0.0, 1.0),
        "block_ids": draw_block_ids(jax.random.fold_in(keys[3], 71), 0),
        "counts": draw_counts(jax.random.fold_in(keys[3], 71), 0),
    }


def filter_valid(padded, along):
    half = (padded.shape[along] - 2) // 2
    terms = [lax.slice_in_dim(padded, offset, offset + 2 * half - 1, 2, along) for offset in range(4)]
    return (terms[0] + 3.0 * terms[1] + 3.0 * terms[2] + terms[3]) * 0.125

def filter_zero(values, along):
    widths = [(0, 0)] * values.ndim
    widths[along] = (1, 1)
    return filter_valid(jnp.pad(values, widths), along)

def cosine_basis():
    index = jnp.arange(8, dtype=jnp.float32)
    weight = jnp.where(index == 0, math.sqrt(1.0 / 8.0), math.sqrt(2.0 / 8.0))
    return weight[:, None] * jnp.cos(math.pi * (2.0 * index[None, :] + 1.0) * index[:, None] / 16.0)

def reference(volume, block_ids, counts):
    downsampled = filter_zero(filter_zero(filter_zero(volume, 0), 1), 2)
    centered = downsampled - 0.5
    blocks = centered.reshape(GROUP // 16, 8, COLUMNS // 16, 8, YROWS // 16, 8)
    basis = cosine_basis()
    spectra = jnp.einsum('zaxbyc,ua,vb,wc->zxyuvw', blocks, basis, basis, basis, precision=lax.Precision.HIGHEST)
    per_col = COLS_DEV // 16
    per_row = ROWS // 16
    depth_idx = block_ids // (per_col * per_row)
    col_idx = jnp.arange(N_SEC, dtype=jnp.int32)[:, None, None] * per_col + block_ids // per_row % per_col
    row_idx = jnp.arange(N_YB, dtype=jnp.int32)[None, :, None] * per_row + block_ids % per_row
    picked = spectra[depth_idx, col_idx, row_idx].reshape(N_SEC, N_YB, SLOTS, 512)
    live = jnp.arange(SLOTS, dtype=jnp.int32)[None, None, :] < counts[:, :, None]
    coeffs = jnp.where(live[..., None], picked, jnp.zeros((), picked.dtype))
    return (downsampled, coeffs)
```

```python
import functools
import math

import jax
import jax.numpy as jnp
import numpy as np
from jax import lax
from jax.experimental import pallas as pl
from jax.experimental.pallas import tpu as pltpu
from jax.sharding import PartitionSpec as P

F32 = jnp.float32
BF16 = jnp.bfloat16
MESH = pl.DeviceIdType.MESH
NY, NZ = 4, 16
N_SEC = NY * NZ
N_YB = 8
COLS = 2048
ROWS = 256
HALF = 128
OUT_COLS = 16
DEPTH = 32
CHUNKS = 8
PAD = 8
SELF_STEP = N_SEC - NY


def cosine_matrix():
    index = np.arange(8, dtype=np.float64)
    weight = np.where(index == 0, math.sqrt(1.0 / 8.0), math.sqrt(2.0 / 8.0))
    basis = weight[:, None] * np.cos(math.pi * (2.0 * index[None, :] + 1.0) * index[:, None] / 16.0)
    return np.einsum("ua,vb,wc->cabuvw", basis, basis, basis).reshape(512, 512).astype(np.float32)


def row_matrix(half):
    inputs = lax.broadcasted_iota(jnp.int32, (HALF, HALF), 0) + half * HALF
    outputs = lax.broadcasted_iota(jnp.int32, (HALF, HALF), 1)
    offset = inputs - (2 * outputs - 1)
    weight = jnp.where((offset == 0) | (offset == 3), 0.125, 0.375)
    return jnp.where((offset >= 0) & (offset <= 3), weight, 0.0).astype(BF16)


def pieces(value):
    high = value.astype(BF16)
    rest = value - high.astype(F32)
    mid = rest.astype(BF16)
    return high, mid, (rest - mid.astype(F32)).astype(BF16)


def kernel(
    x_hbm, ids_ref, cnt_ref, k_hbm, ds_ref, co_ref,
    xbuf, plane, stacked, k_full, k_ref, turned, edge_out, edge_in,
    x_sem, k_sem, send_sem, recv_sem, edge_send, edge_recv,
):
    me = lax.axis_index("sec")
    band = lax.axis_index("yb")
    y, z = me // NZ, me % NZ
    size = COLS // CHUNKS
    out_size = size // 2

    def load(chunk, half):
        return pltpu.make_async_copy(
            x_hbm.at[pl.ds(chunk * size, size), pl.ds(half * HALF, HALF)],
            xbuf.at[half, pl.ds(PAD + chunk * size, size), :],
            x_sem.at[chunk, half],
        )

    edge_in[...] = jnp.zeros(edge_in.shape, F32)
    for chunk in range(CHUNKS):
        for half in range(2):
            load(chunk, half).start()
    basis_copy = pltpu.make_async_copy(k_hbm, k_full, k_sem)
    basis_copy.start()

    def peer(step):
        dy, turn = step % NY, step // NY
        hop = turn // 2
        dz = jnp.where(turn % 2 == 0, NZ // 2 - hop, hop - (NZ // 2 - 1))
        return ((y + dy) % NY) * NZ + (z + dz + NZ) % NZ

    def source(step):
        dy, turn = step % NY, step // NY
        hop = turn // 2
        dz = jnp.where(turn % 2 == 0, NZ // 2 - hop, hop - (NZ // 2 - 1))
        return ((y - dy + NY) % NY) * NZ + (z - dz + NZ) % NZ

    barrier = pltpu.get_barrier_semaphore()

    def greet(step, carry):
        pl.semaphore_signal(barrier, inc=1, device_id=(peer(step), band), device_id_type=MESH)
        return carry

    lax.fori_loop(0, SELF_STEP, greet, 0)
    lax.fori_loop(SELF_STEP + 1, N_SEC, greet, 0)

    @pl.when(band > 0)
    def _():
        pl.semaphore_signal(barrier, inc=1, device_id=(me, band - 1), device_id_type=MESH)

    @pl.when(band < N_YB - 1)
    def _():
        pl.semaphore_signal(barrier, inc=1, device_id=(me, band + 1), device_id_type=MESH)

    for half in range(2):
        xbuf[half, pl.ds(0, PAD), :] = jnp.zeros((PAD, HALF), F32)
        xbuf[half, pl.ds(PAD + COLS, PAD), :] = jnp.zeros((PAD, HALF), F32)

    lane = lax.broadcasted_iota(jnp.int32, (8, HALF), 1)
    row_weights = [row_matrix(half) for half in range(2)]
    first_row = jnp.zeros((8, HALF), F32)
    last_row = jnp.zeros((8, HALF), F32)
    for half in range(2):
        load(0, half).wait()
    for chunk in range(CHUNKS):
        if chunk + 1 < CHUNKS:
            for half in range(2):
                load(chunk + 1, half).wait()
        total = jnp.zeros((out_size, HALF), F32)
        for half in range(2):
            start = PAD + chunk * size - 1
            taps = [xbuf[half, pl.ds(start + a, out_size, stride=2), :] for a in range(4)]
            narrow = (taps[0] + taps[3] + 3.0 * (taps[1] + taps[2])) * 0.125
            for part in pieces(narrow):
                total += jnp.dot(
                    part, row_weights[half], preferred_element_type=F32
                )
            for inner in range(out_size // 8):
                group = chunk * (out_size // 8) + inner
                rows = narrow[inner * 8 : inner * 8 + 8, :]
                if half == 0:
                    moved = rows if group == 0 else pltpu.roll(rows, group, 1)
                    first_row = jnp.where(lane == group, moved, first_row)
                else:
                    shift = (group + 1) % HALF
                    moved = rows if shift == 0 else pltpu.roll(rows, shift, 1)
                    last_row = jnp.where(lane == group, moved, last_row)
        per = out_size // OUT_COLS
        plane[pl.ds(chunk * per, per)] = total.reshape(per, OUT_COLS, HALF)
    edge_out[0] = first_row * 0.125
    edge_out[1] = last_row * 0.125

    inside = (band > 0).astype(jnp.int32) + (band < N_YB - 1).astype(jnp.int32)
    pl.semaphore_wait(barrier, N_SEC - 1 + inside)

    def edge_copy(which, target):
        return pltpu.make_async_remote_copy(
            src_ref=edge_out.at[which],
            dst_ref=edge_in.at[which],
            send_sem=edge_send.at[which],
            recv_sem=edge_recv.at[which],
            device_id=(me, target),
            device_id_type=MESH,
        )

    @pl.when(band > 0)
    def _():
        edge_copy(0, band - 1).start()

    @pl.when(band < N_YB - 1)
    def _():
        edge_copy(1, band + 1).start()

    @pl.when(band < N_YB - 1)
    def _():
        edge_copy(0, band + 1).wait_recv()

    @pl.when(band > 0)
    def _():
        edge_copy(1, band - 1).wait_recv()

    above, below = edge_in[0], edge_in[1]

    def finished(target):
        parts = []
        for sub in range(2):
            group = 2 * target + sub
            low = pltpu.roll(below, (HALF - group) % HALF, 1)
            high = pltpu.roll(above, (2 * HALF - 1 - group) % HALF, 1)
            rows = plane[target, pl.ds(sub * 8, 8), :]
            parts.append(
                rows + jnp.where(lane == 0, low, 0.0) + jnp.where(lane == HALF - 1, high, 0.0)
            )
        return parts

    def chunk_copy(target, slot):
        return pltpu.make_async_remote_copy(
            src_ref=plane.at[target],
            dst_ref=stacked.at[slot],
            send_sem=send_sem,
            recv_sem=recv_sem.at[slot],
            device_id=(target, band),
            device_id_type=MESH,
        )

    def send(step, carry):
        target = peer(step)
        for sub, rows in enumerate(finished(target)):
            plane[target, pl.ds(sub * 8, 8), :] = rows
        chunk_copy(target, me).start()
        return carry

    lax.fori_loop(0, SELF_STEP, send, 0)
    lax.fori_loop(SELF_STEP + 1, N_SEC, send, 0)
    for sub, rows in enumerate(finished(me)):
        stacked[me, pl.ds(sub * 8, 8), :] = rows
    basis_copy.wait()
    k_ref[0] = k_full[...].astype(BF16)
    k_ref[1] = (k_full[...] - k_ref[0].astype(F32)).astype(BF16)

    def receive(step, carry):
        origin = source(step)
        chunk_copy(origin, origin).wait_recv()
        return carry

    lax.fori_loop(0, SELF_STEP, receive, 0)
    lax.fori_loop(SELF_STEP + 1, N_SEC, receive, 0)

    for bz in range(DEPTH // 8):
        for k in range(8 * bz, 8 * bz + 8):
            value = 3.0 * (stacked[2 * k] + stacked[2 * k + 1])
            if k > 0:
                value += stacked[2 * k - 1]
            if k < DEPTH - 1:
                value += stacked[2 * k + 2]
            ds_ref[k] = value * 0.125
        group = ds_ref[pl.ds(8 * bz, 8)] - 0.5
        flat = jnp.concatenate(
            [group[:, 0:8, :].reshape(64, HALF), group[:, 8:16, :].reshape(64, HALF)], axis=0
        )
        turned[bz] = flat.T

    wide = lax.broadcasted_iota(jnp.int32, (16, HALF), 1)
    tiles = []
    for pair in range(4):
        rows = []
        for bz in range(DEPTH // 8):
            even = turned[bz, pl.ds(2 * pair, 16, stride=8), :]
            odd = turned[bz, pl.ds(2 * pair + 1, 16, stride=8), :]
            rows.append(jnp.where(wide < 64, even, pltpu.roll(odd, 64, 1)))
            rows.append(jnp.where(wide < 64, pltpu.roll(even, 64, 1), odd))
        tiles.append(jnp.concatenate(rows, axis=0))
    blocks = jnp.concatenate(tiles, axis=1)
    high = blocks.astype(BF16)
    low = (blocks - high.astype(F32)).astype(BF16)
    number = lax.broadcasted_iota(jnp.int32, (HALF, 64), 0)
    slot = lax.broadcasted_iota(jnp.int32, (HALF, 64), 1)
    chosen = (number == ids_ref[...]) & (slot < cnt_ref[0, 0])
    chosen = jnp.where(chosen, 1.0, 0.0).T.astype(BF16)
    high = jnp.dot(chosen, high, preferred_element_type=F32).astype(BF16)
    low = jnp.dot(chosen, low, preferred_element_type=F32).astype(BF16)
    co_ref[...] = (
        jnp.dot(high, k_ref[0], preferred_element_type=F32)
        + jnp.dot(low, k_ref[0], preferred_element_type=F32)
        + jnp.dot(high, k_ref[1], preferred_element_type=F32)
    )

    pltpu.make_async_remote_copy(
        src_ref=plane.at[pl.ds(0, N_SEC - 1)],
        dst_ref=stacked.at[pl.ds(0, N_SEC - 1)],
        send_sem=send_sem,
        recv_sem=recv_sem.at[0],
        device_id=(peer(0), band),
        device_id_type=MESH,
    ).wait_send()

    @pl.when(band > 0)
    def _():
        edge_copy(0, band - 1).wait_send()

    @pl.when(band < N_YB - 1)
    def _():
        edge_copy(1, band + 1).wait_send()


def on_device(volume, block_ids, counts):
    section = volume.reshape(COLS, ROWS)
    vmem = pl.BlockSpec(memory_space=pltpu.VMEM)
    hbm = pl.BlockSpec(memory_space=pl.ANY)
    downsampled, coeffs = pl.pallas_call(
        kernel,
        out_shape=(
            jax.ShapeDtypeStruct((DEPTH, OUT_COLS, HALF), F32),
            jax.ShapeDtypeStruct((64, 512), F32),
        ),
        in_specs=[hbm, vmem, pl.BlockSpec(memory_space=pltpu.SMEM), hbm],
        out_specs=(vmem, vmem),
        scratch_shapes=[
            pltpu.VMEM((2, COLS + 2 * PAD, HALF), F32),
            pltpu.VMEM((N_SEC, OUT_COLS, HALF), F32),
            pltpu.VMEM((N_SEC, OUT_COLS, HALF), F32),
            pltpu.VMEM((512, 512), F32),
            pltpu.VMEM((2, 512, 512), BF16),
            pltpu.VMEM((4, HALF, HALF), F32),
            pltpu.VMEM((2, 8, HALF), F32),
            pltpu.VMEM((2, 8, HALF), F32),
            pltpu.SemaphoreType.DMA((CHUNKS, 2)),
            pltpu.SemaphoreType.DMA,
            pltpu.SemaphoreType.DMA,
            pltpu.SemaphoreType.DMA((N_SEC,)),
            pltpu.SemaphoreType.DMA((2,)),
            pltpu.SemaphoreType.DMA((2,)),
        ],
        compiler_params=pltpu.CompilerParams(
            collective_id=0, has_side_effects=True, vmem_limit_bytes=60 * 1024 * 1024
        ),
    )(section, block_ids.reshape(1, 64), counts, jnp.asarray(cosine_matrix()))
    return downsampled, coeffs.reshape(1, 1, 64, 512)


def solution(mesh):
    placed = (P("sec", None, "yb"), P("sec", "yb", None), P("sec", "yb"))
    return jax.shard_map(
        on_device,
        mesh=mesh,
        in_specs=placed,
        out_specs=(P(None, "sec", "yb"), P("sec", "yb", None, None)),
        check_vma=False,
    )
```

```python
import functools
import math

import jax
import jax.numpy as jnp
import numpy as np
from jax import lax
from jax.experimental import pallas as pl
from jax.experimental.pallas import tpu as pltpu
from jax.sharding import PartitionSpec as P

F32 = jnp.float32
BF16 = jnp.bfloat16
MESH = pl.DeviceIdType.MESH
NY, NZ = 4, 16
N_SEC = NY * NZ
N_YB = 8
COLS = 2048
ROWS = 256
HALF = 128
OUT_COLS = 16
DEPTH = 32
CHUNKS = 8
PAD = 8
GROUP_Z = NZ // 2
WINDOW = 2
OWN_ROUND = 3
OWN_ROUNDS = 4


def cosine_matrix():
    index = np.arange(8, dtype=np.float64)
    weight = np.where(index == 0, math.sqrt(1.0 / 8.0), math.sqrt(2.0 / 8.0))
    basis = weight[:, None] * np.cos(math.pi * (2.0 * index[None, :] + 1.0) * index[:, None] / 16.0)
    return np.einsum("ua,vb,wc->cabuvw", basis, basis, basis).reshape(512, 512).astype(np.float32)


def row_matrix(half):
    inputs = lax.broadcasted_iota(jnp.int32, (HALF, HALF), 0) + half * HALF
    outputs = lax.broadcasted_iota(jnp.int32, (HALF, HALF), 1)
    offset = inputs - (2 * outputs - 1)
    weight = jnp.where((offset == 0) | (offset == 3), 0.125, 0.375)
    return jnp.where((offset >= 0) & (offset <= 3), weight, 0.0).astype(BF16)


def pieces(value):
    high = value.astype(BF16)
    rest = value - high.astype(F32)
    mid = rest.astype(BF16)
    return high, mid, (rest - mid.astype(F32)).astype(BF16)


def kernel(
    x_hbm, ids_ref, cnt_ref, k_hbm, ds_ref, co_ref,
    xbuf, plane, stacked, k_full, k_ref, turned, edge_out, edge_in,
    x_sem, k_sem, send_sem, recv_sem, edge_send, edge_recv, late_sem, up_sem, down_sem,
):
    me = lax.axis_index("sec")
    band = lax.axis_index("yb")
    y, z = me // NZ, me % NZ
    size = COLS // CHUNKS
    out_size = size // 2

    def load(chunk, half):
        return pltpu.make_async_copy(
            x_hbm.at[pl.ds(chunk * size, size), pl.ds(half * HALF, HALF)],
            xbuf.at[half, pl.ds(PAD + chunk * size, size), :],
            x_sem.at[chunk, half],
        )

    edge_in[...] = jnp.zeros(edge_in.shape, F32)
    for chunk in range(CHUNKS):
        for half in range(2):
            load(chunk, half).start()
    basis_copy = pltpu.make_async_copy(k_hbm, k_full, k_sem)
    basis_copy.start()

    late = z >= GROUP_Z

    def signal(semaphore, column, row):
        pl.semaphore_signal(semaphore, inc=1, device_id=(column, row), device_id_type=MESH)

    def visit_group(visit, own):
        def step(index, carry):
            turn, dy = index // NY, index % NY
            hop = turn // 2
            dz = jnp.where(turn % 2 == 0, NZ // 2 - hop, hop - (NZ // 2 - 1))
            target = (z + dz + NZ) % NZ
            same = (target >= GROUP_Z) == late

            @pl.when(same if own else jnp.logical_not(same))
            def _():
                visit(((y + dy) % NY) * NZ + target)

            return carry

        lax.fori_loop(0, NY * (NZ - 1), step, 0)
        if own:
            for dy in range(1, NY):
                visit(((y + dy) % NY) * NZ + z)

    barrier = pltpu.get_barrier_semaphore()

    @pl.when(band > 0)
    def _():
        signal(barrier, me, band - 1)

    @pl.when(band < N_YB - 1)
    def _():
        signal(barrier, me, band + 1)

    @pl.when(jnp.logical_not(late))
    def _():
        visit_group(lambda column: signal(barrier, column, band), False)
        visit_group(lambda column: signal(barrier, column, band), True)

    for half in range(2):
        xbuf[half, pl.ds(0, PAD), :] = jnp.zeros((PAD, HALF), F32)
        xbuf[half, pl.ds(PAD + COLS, PAD), :] = jnp.zeros((PAD, HALF), F32)

    lane = lax.broadcasted_iota(jnp.int32, (8, HALF), 1)
    row_weights = [row_matrix(half) for half in range(2)]
    first_row = jnp.zeros((8, HALF), F32)
    last_row = jnp.zeros((8, HALF), F32)
    for half in range(2):
        load(0, half).wait()
    for chunk in range(CHUNKS):
        if chunk + 1 < CHUNKS:
            for half in range(2):
                load(chunk + 1, half).wait()
        total = jnp.zeros((out_size, HALF), F32)
        for half in range(2):
            start = PAD + chunk * size - 1
            taps = [xbuf[half, pl.ds(start + a, out_size, stride=2), :] for a in range(4)]
            narrow = (taps[0] + taps[3] + 3.0 * (taps[1] + taps[2])) * 0.125
            for part in pieces(narrow):
                total += jnp.dot(
                    part, row_weights[half], preferred_element_type=F32
                )
            for inner in range(out_size // 8):
                group = chunk * (out_size // 8) + inner
                rows = narrow[inner * 8 : inner * 8 + 8, :]
                if half == 0:
                    moved = rows if group == 0 else pltpu.roll(rows, group, 1)
                    first_row = jnp.where(lane == group, moved, first_row)
                else:
                    shift = (group + 1) % HALF
                    moved = rows if shift == 0 else pltpu.roll(rows, shift, 1)
                    last_row = jnp.where(lane == group, moved, last_row)
        per = out_size // OUT_COLS
        plane[pl.ds(chunk * per, per)] = total.reshape(per, OUT_COLS, HALF)
    edge_out[0] = first_row * 0.125
    edge_out[1] = last_row * 0.125

    inside = (band > 0).astype(jnp.int32) + (band < N_YB - 1).astype(jnp.int32)
    pl.semaphore_wait(barrier, NY * GROUP_Z - 1 + inside + late.astype(jnp.int32))

    def edge_copy(which, target):
        return pltpu.make_async_remote_copy(
            src_ref=edge_out.at[which],
            dst_ref=edge_in.at[which],
            send_sem=edge_send.at[which],
            recv_sem=edge_recv.at[which],
            device_id=(me, target),
            device_id_type=MESH,
        )

    @pl.when(band > 0)
    def _():
        edge_copy(0, band - 1).start()

    @pl.when(band < N_YB - 1)
    def _():
        edge_copy(1, band + 1).start()

    @pl.when(late)
    def _():
        visit_group(lambda column: signal(late_sem, column, band), False)

    @pl.when(band < N_YB - 1)
    def _():
        edge_copy(0, band + 1).wait_recv()

    @pl.when(band > 0)
    def _():
        edge_copy(1, band - 1).wait_recv()

    above, below = edge_in[0], edge_in[1]

    for group in range(COLS // 16):
        low = below if group == 0 else pltpu.roll(below, HALF - group, 1)
        high = above if group == HALF - 1 else pltpu.roll(above, HALF - 1 - group, 1)
        rows = pl.ds(group % 2 * 8, 8)
        plane[group // 2, rows, :] += jnp.where(lane == 0, low, 0.0) + jnp.where(
            lane == HALF - 1, high, 0.0
        )

    def chunk_copy(target, slot, semaphore=send_sem):
        return pltpu.make_async_remote_copy(
            src_ref=plane.at[target],
            dst_ref=stacked.at[slot],
            send_sem=semaphore,
            recv_sem=recv_sem.at[slot],
            device_id=(target, band),
            device_id_type=MESH,
        )

    def send(target):
        chunk_copy(target, me).start()

    stacked[me] = plane[me]

    def sent(semaphore, count):
        pltpu.make_async_remote_copy(
            src_ref=plane.at[pl.ds(0, count)],
            dst_ref=stacked.at[pl.ds(0, count)],
            send_sem=semaphore,
            recv_sem=recv_sem.at[0],
            device_id=((me + 1) % N_SEC, band),
            device_id_type=MESH,
        ).wait_send()

    place = z - GROUP_Z

    def sent_round(index):
        @pl.when(index < place)
        def _():
            sent(up_sem.at[index], NY)

        @pl.when(index + place < GROUP_Z)
        def _():
            sent(down_sem.at[index], NY)

    def send_round(index, carry):
        @pl.when(index >= WINDOW)
        def _():
            sent_round(index - WINDOW)

        for dy in range(NY):
            column = ((y + dy) % NY) * NZ

            @pl.when(index < place)
            def _():
                chunk_copy(column + index, me, up_sem.at[index]).start()

            @pl.when(index + place < GROUP_Z)
            def _():
                chunk_copy(column + place + index, me, down_sem.at[index]).start()

        @pl.when(index == OWN_ROUND)
        def _():
            pl.semaphore_wait(late_sem, 1)

        @pl.when((index >= OWN_ROUND) & (index < OWN_ROUND + OWN_ROUNDS))
        def _():
            for half in range(GROUP_Z // OWN_ROUNDS):
                turn = (index - OWN_ROUND) * (GROUP_Z // OWN_ROUNDS) + half
                target = GROUP_Z + (place + turn) % GROUP_Z

                @pl.when(turn > 0)
                def _():
                    send(y * NZ + target)

                for dy in range(1, NY):
                    send(((y + dy) % NY) * NZ + target)

        return carry

    @pl.when(late)
    def _():
        lax.fori_loop(0, GROUP_Z, send_round, 0)
        for index in range(GROUP_Z - WINDOW, GROUP_Z):
            sent_round(index)

    @pl.when(jnp.logical_not(late))
    def _():
        visit_group(send, True)
        pl.semaphore_wait(late_sem, NY * GROUP_Z)
        signal(late_sem, me + GROUP_Z, band)
        visit_group(send, False)

    basis_copy.wait()
    k_ref[0] = k_full[...].astype(BF16)
    k_ref[1] = (k_full[...] - k_ref[0].astype(F32)).astype(BF16)

    def receive(step, carry):
        origin = (me + step) % N_SEC
        chunk_copy(origin, origin).wait_recv()
        return carry

    lax.fori_loop(1, N_SEC, receive, 0)

    for bz in range(DEPTH // 8):
        for k in range(8 * bz, 8 * bz + 8):
            value = 3.0 * (stacked[2 * k] + stacked[2 * k + 1])
            if k > 0:
                value += stacked[2 * k - 1]
            if k < DEPTH - 1:
                value += stacked[2 * k + 2]
            ds_ref[k] = value * 0.125
        group = ds_ref[pl.ds(8 * bz, 8)] - 0.5
        flat = jnp.concatenate(
            [group[:, 0:8, :].reshape(64, HALF), group[:, 8:16, :].reshape(64, HALF)], axis=0
        )
        turned[bz] = flat.T

    wide = lax.broadcasted_iota(jnp.int32, (16, HALF), 1)
    tiles = []
    for pair in range(4):
        rows = []
        for bz in range(DEPTH // 8):
            even = turned[bz, pl.ds(2 * pair, 16, stride=8), :]
            odd = turned[bz, pl.ds(2 * pair + 1, 16, stride=8), :]
            rows.append(jnp.where(wide < 64, even, pltpu.roll(odd, 64, 1)))
            rows.append(jnp.where(wide < 64, pltpu.roll(even, 64, 1), odd))
        tiles.append(jnp.concatenate(rows, axis=0))
    blocks = jnp.concatenate(tiles, axis=1)
    high = blocks.astype(BF16)
    low = (blocks - high.astype(F32)).astype(BF16)
    row = lax.broadcasted_iota(jnp.int32, (8, HALF), 0)
    picks = []
    for first in range(0, 64, 8):
        number = jnp.full((8, HALF), -1, jnp.int32)
        for slot in range(8):
            live = jnp.where(first + slot < cnt_ref[0, 0], ids_ref[0, first + slot], -1)
            number = jnp.where(row == slot, live, number)
        picks.append(jnp.where(number == lane, 1.0, 0.0))
    chosen = jnp.concatenate(picks, axis=0).astype(BF16)
    high = jnp.dot(chosen, high, preferred_element_type=F32).astype(BF16)
    low = jnp.dot(chosen, low, preferred_element_type=F32).astype(BF16)
    co_ref[...] = (
        jnp.dot(high, k_ref[0], preferred_element_type=F32)
        + jnp.dot(low, k_ref[0], preferred_element_type=F32)
        + jnp.dot(high, k_ref[1], preferred_element_type=F32)
    )

    sent(send_sem, NY * GROUP_Z - 1)

    @pl.when(jnp.logical_not(late))
    def _():
        sent(send_sem, NY * GROUP_Z)

    @pl.when(band > 0)
    def _():
        edge_copy(0, band - 1).wait_send()

    @pl.when(band < N_YB - 1)
    def _():
        edge_copy(1, band + 1).wait_send()


def on_device(volume, block_ids, counts):
    section = volume.reshape(COLS, ROWS)
    vmem = pl.BlockSpec(memory_space=pltpu.VMEM)
    smem = pl.BlockSpec(memory_space=pltpu.SMEM)
    hbm = pl.BlockSpec(memory_space=pl.ANY)
    downsampled, coeffs = pl.pallas_call(
        kernel,
        out_shape=(
            jax.ShapeDtypeStruct((DEPTH, OUT_COLS, HALF), F32),
            jax.ShapeDtypeStruct((64, 512), F32),
        ),
        in_specs=[hbm, smem, smem, hbm],
        out_specs=(vmem, vmem),
        scratch_shapes=[
            pltpu.VMEM((2, COLS + 2 * PAD, HALF), F32),
            pltpu.VMEM((N_SEC, OUT_COLS, HALF), F32),
            pltpu.VMEM((N_SEC, OUT_COLS, HALF), F32),
            pltpu.VMEM((512, 512), F32),
            pltpu.VMEM((2, 512, 512), BF16),
            pltpu.VMEM((4, HALF, HALF), F32),
            pltpu.VMEM((2, 8, HALF), F32),
            pltpu.VMEM((2, 8, HALF), F32),
            pltpu.SemaphoreType.DMA((CHUNKS, 2)),
            pltpu.SemaphoreType.DMA,
            pltpu.SemaphoreType.DMA,
            pltpu.SemaphoreType.DMA((N_SEC,)),
            pltpu.SemaphoreType.DMA((2,)),
            pltpu.SemaphoreType.DMA((2,)),
            pltpu.SemaphoreType.REGULAR,
            pltpu.SemaphoreType.DMA((GROUP_Z,)),
            pltpu.SemaphoreType.DMA((GROUP_Z,)),
        ],
        compiler_params=pltpu.CompilerParams(
            collective_id=0, has_side_effects=True, vmem_limit_bytes=53 * 1024 * 1024
        ),
    )(section, block_ids.reshape(1, 64), counts, jnp.asarray(cosine_matrix()))
    return downsampled, coeffs.reshape(1, 1, 64, 512)


def solution(mesh):
    placed = (P("sec", None, "yb"), P("sec", "yb", None), P("sec", "yb"))
    return jax.shard_map(
        on_device,
        mesh=mesh,
        in_specs=placed,
        out_specs=(P(None, "sec", "yb"), P("sec", "yb", None, None)),
        check_vma=False,
    )
```

```python
import functools
import math

import jax
import jax.numpy as jnp
from jax import lax
from jax.experimental import pallas as pl
from jax.experimental.pallas import tpu as pltpu
from jax.sharding import PartitionSpec as P

F32 = jnp.float32
BF16 = jnp.bfloat16
MESH = pl.DeviceIdType.MESH
NY, NZ = 4, 16
N_SEC = NY * NZ
N_YB = 8
COLS = 2048
ROWS = 256
HALF = 128
OUT_COLS = 16
DEPTH = 32
CHUNKS = 8
PAD = 8
GROUP_Z = NZ // 2
WINDOW = 2
OWN_ROUND = 3
OWN_ROUNDS = 4


def cosines(frequency, place):
    turn = ((2 * place + 1) * frequency) % 32
    value = jnp.zeros(turn.shape, F32)
    for step in range(32):
        value = jnp.where(turn == step, math.cos(math.pi * step / 16.0), value)
    return value * jnp.where(frequency == 0, math.sqrt(1.0 / 8.0), math.sqrt(2.0 / 8.0))


def fill_basis(k_ref):
    place = lax.broadcasted_iota(jnp.int32, (8, 512), 0)
    output = lax.broadcasted_iota(jnp.int32, (8, 512), 1)
    along_depth = cosines(output // 64, place)
    along_column = cosines(output // 8 % 8, place)
    along_row = cosines(output % 8, place)
    for c in range(8):
        for a in range(0, 8, 2):
            parts = [
                along_column * (along_row[c : c + 1, :] * along_depth[a + i : a + i + 1, :])
                for i in range(2)
            ]
            value = jnp.concatenate(parts, axis=0)
            high = value.astype(BF16)
            rows = pl.ds(64 * c + 8 * a, 16)
            k_ref[0, rows, :] = high
            k_ref[1, rows, :] = (value - high.astype(F32)).astype(BF16)


def row_matrix(half):
    inputs = lax.broadcasted_iota(jnp.int32, (HALF, HALF), 0) + half * HALF
    outputs = lax.broadcasted_iota(jnp.int32, (HALF, HALF), 1)
    offset = inputs - (2 * outputs - 1)
    weight = jnp.where((offset == 0) | (offset == 3), 0.125, 0.375)
    return jnp.where((offset >= 0) & (offset <= 3), weight, 0.0).astype(BF16)


def pieces(value):
    high = value.astype(BF16)
    rest = value - high.astype(F32)
    mid = rest.astype(BF16)
    return high, mid, (rest - mid.astype(F32)).astype(BF16)


def exchange(
    x_hbm, stacked, k_ref,
    xbuf, plane, edge_out, edge_in,
    x_sem, send_sem, recv_sem, edge_send, edge_recv, late_sem, up_sem, down_sem,
):
    me = lax.axis_index("sec")
    band = lax.axis_index("yb")
    y, z = me // NZ, me % NZ
    size = COLS // CHUNKS
    out_size = size // 2

    def load(chunk, half):
        return pltpu.make_async_copy(
            x_hbm.at[pl.ds(chunk * size, size), pl.ds(half * HALF, HALF)],
            xbuf.at[half, pl.ds(PAD + chunk * size, size), :],
            x_sem.at[chunk, half],
        )

    edge_in[...] = jnp.zeros(edge_in.shape, F32)
    for chunk in range(CHUNKS):
        for half in range(2):
            load(chunk, half).start()

    late = z >= GROUP_Z

    def signal(semaphore, column, row):
        pl.semaphore_signal(semaphore, inc=1, device_id=(column, row), device_id_type=MESH)

    def visit_group(visit, own):
        def step(index, carry):
            turn, dy = index // NY, index % NY
            hop = turn // 2
            dz = jnp.where(turn % 2 == 0, NZ // 2 - hop, hop - (NZ // 2 - 1))
            target = (z + dz + NZ) % NZ
            same = (target >= GROUP_Z) == late

            @pl.when(same if own else jnp.logical_not(same))
            def _():
                visit(((y + dy) % NY) * NZ + target)

            return carry

        lax.fori_loop(0, NY * (NZ - 1), step, 0)
        if own:
            for dy in range(1, NY):
                visit(((y + dy) % NY) * NZ + z)

    barrier = pltpu.get_barrier_semaphore()

    @pl.when(band > 0)
    def _():
        signal(barrier, me, band - 1)

    @pl.when(band < N_YB - 1)
    def _():
        signal(barrier, me, band + 1)

    @pl.when(jnp.logical_not(late))
    def _():
        visit_group(lambda column: signal(barrier, column, band), False)
        visit_group(lambda column: signal(barrier, column, band), True)

    for half in range(2):
        xbuf[half, pl.ds(0, PAD), :] = jnp.zeros((PAD, HALF), F32)
        xbuf[half, pl.ds(PAD + COLS, PAD), :] = jnp.zeros((PAD, HALF), F32)

    lane = lax.broadcasted_iota(jnp.int32, (8, HALF), 1)
    row_weights = [row_matrix(half) for half in range(2)]
    first_row = jnp.zeros((8, HALF), F32)
    last_row = jnp.zeros((8, HALF), F32)
    for half in range(2):
        load(0, half).wait()
    for chunk in range(CHUNKS):
        if chunk + 1 < CHUNKS:
            for half in range(2):
                load(chunk + 1, half).wait()
        total = jnp.zeros((out_size, HALF), F32)
        for half in range(2):
            start = PAD + chunk * size - 1
            taps = [xbuf[half, pl.ds(start + a, out_size, stride=2), :] for a in range(4)]
            narrow = (taps[0] + taps[3] + 3.0 * (taps[1] + taps[2])) * 0.125
            for part in pieces(narrow):
                total += jnp.dot(
                    part, row_weights[half], preferred_element_type=F32
                )
            for inner in range(out_size // 8):
                group = chunk * (out_size // 8) + inner
                rows = narrow[inner * 8 : inner * 8 + 8, :]
                if half == 0:
                    moved = rows if group == 0 else pltpu.roll(rows, group, 1)
                    first_row = jnp.where(lane == group, moved, first_row)
                else:
                    shift = (group + 1) % HALF
                    moved = rows if shift == 0 else pltpu.roll(rows, shift, 1)
                    last_row = jnp.where(lane == group, moved, last_row)
        per = out_size // OUT_COLS
        plane[pl.ds(chunk * per, per)] = total.reshape(per, OUT_COLS, HALF)
    edge_out[0] = first_row * 0.125
    edge_out[1] = last_row * 0.125

    inside = (band > 0).astype(jnp.int32) + (band < N_YB - 1).astype(jnp.int32)
    pl.semaphore_wait(barrier, NY * GROUP_Z - 1 + inside + late.astype(jnp.int32))

    def edge_copy(which, target):
        return pltpu.make_async_remote_copy(
            src_ref=edge_out.at[which],
            dst_ref=edge_in.at[which],
            send_sem=edge_send.at[which],
            recv_sem=edge_recv.at[which],
            device_id=(me, target),
            device_id_type=MESH,
        )

    @pl.when(band > 0)
    def _():
        edge_copy(0, band - 1).start()

    @pl.when(band < N_YB - 1)
    def _():
        edge_copy(1, band + 1).start()

    @pl.when(late)
    def _():
        visit_group(lambda column: signal(late_sem, column, band), False)

    @pl.when(band < N_YB - 1)
    def _():
        edge_copy(0, band + 1).wait_recv()

    @pl.when(band > 0)
    def _():
        edge_copy(1, band - 1).wait_recv()

    above, below = edge_in[0], edge_in[1]

    for group in range(COLS // 16):
        low = below if group == 0 else pltpu.roll(below, HALF - group, 1)
        high = above if group == HALF - 1 else pltpu.roll(above, HALF - 1 - group, 1)
        rows = pl.ds(group % 2 * 8, 8)
        plane[group // 2, rows, :] += jnp.where(lane == 0, low, 0.0) + jnp.where(
            lane == HALF - 1, high, 0.0
        )

    def chunk_copy(target, slot, semaphore=send_sem):
        return pltpu.make_async_remote_copy(
            src_ref=plane.at[target],
            dst_ref=stacked.at[slot],
            send_sem=semaphore,
            recv_sem=recv_sem.at[slot],
            device_id=(target, band),
            device_id_type=MESH,
        )

    def send(target):
        chunk_copy(target, me).start()

    stacked[me] = plane[me]

    def sent(semaphore, count):
        pltpu.make_async_remote_copy(
            src_ref=plane.at[pl.ds(0, count)],
            dst_ref=stacked.at[pl.ds(0, count)],
            send_sem=semaphore,
            recv_sem=recv_sem.at[0],
            device_id=((me + 1) % N_SEC, band),
            device_id_type=MESH,
        ).wait_send()

    place = z - GROUP_Z

    def sent_round(index):
        @pl.when(index < place)
        def _():
            sent(up_sem.at[index], NY)

        @pl.when(index + place < GROUP_Z)
        def _():
            sent(down_sem.at[index], NY)

    def send_round(index, carry):
        @pl.when(index >= WINDOW)
        def _():
            sent_round(index - WINDOW)

        for dy in range(NY):
            column = ((y + dy) % NY) * NZ

            @pl.when(index < place)
            def _():
                chunk_copy(column + index, me, up_sem.at[index]).start()

            @pl.when(index + place < GROUP_Z)
            def _():
                chunk_copy(column + place + index, me, down_sem.at[index]).start()

        @pl.when(index == OWN_ROUND)
        def _():
            pl.semaphore_wait(late_sem, 1)

        @pl.when((index >= OWN_ROUND) & (index < OWN_ROUND + OWN_ROUNDS))
        def _():
            for half in range(GROUP_Z // OWN_ROUNDS):
                turn = (index - OWN_ROUND) * (GROUP_Z // OWN_ROUNDS) + half
                target = GROUP_Z + (place + turn) % GROUP_Z

                @pl.when(turn > 0)
                def _():
                    send(y * NZ + target)

                for dy in range(1, NY):
                    send(((y + dy) % NY) * NZ + target)

        return carry

    @pl.when(late)
    def _():
        lax.fori_loop(0, GROUP_Z, send_round, 0)
        for index in range(GROUP_Z - WINDOW, GROUP_Z):
            sent_round(index)

    @pl.when(jnp.logical_not(late))
    def _():
        visit_group(send, True)
        pl.semaphore_wait(late_sem, NY * GROUP_Z)
        signal(late_sem, me + GROUP_Z, band)
        visit_group(send, False)

    fill_basis(k_ref)

    def receive(step, carry):
        origin = (me + step) % N_SEC
        chunk_copy(origin, origin).wait_recv()
        return carry

    lax.fori_loop(1, N_SEC, receive, 0)

    sent(send_sem, NY * GROUP_Z - 1)

    @pl.when(jnp.logical_not(late))
    def _():
        sent(send_sem, NY * GROUP_Z)

    @pl.when(band > 0)
    def _():
        edge_copy(0, band - 1).wait_send()

    @pl.when(band < N_YB - 1)
    def _():
        edge_copy(1, band + 1).wait_send()


def transform(stacked, k_ref, ids_ref, cnt_ref, ds_ref, co_ref, turned):
    for bz in range(DEPTH // 8):
        for k in range(8 * bz, 8 * bz + 8):
            value = 3.0 * (stacked[2 * k] + stacked[2 * k + 1])
            if k > 0:
                value += stacked[2 * k - 1]
            if k < DEPTH - 1:
                value += stacked[2 * k + 2]
            ds_ref[k] = value * 0.125
        group = ds_ref[pl.ds(8 * bz, 8)] - 0.5
        flat = jnp.concatenate(
            [group[:, 0:8, :].reshape(64, HALF), group[:, 8:16, :].reshape(64, HALF)], axis=0
        )
        turned[bz] = flat.T

    lane = lax.broadcasted_iota(jnp.int32, (8, HALF), 1)
    wide = lax.broadcasted_iota(jnp.int32, (16, HALF), 1)
    tiles = []
    for pair in range(4):
        rows = []
        for bz in range(DEPTH // 8):
            even = turned[bz, pl.ds(2 * pair, 16, stride=8), :]
            odd = turned[bz, pl.ds(2 * pair + 1, 16, stride=8), :]
            rows.append(jnp.where(wide < 64, even, pltpu.roll(odd, 64, 1)))
            rows.append(jnp.where(wide < 64, pltpu.roll(even, 64, 1), odd))
        tiles.append(jnp.concatenate(rows, axis=0))
    blocks = jnp.concatenate(tiles, axis=1)
    high = blocks.astype(BF16)
    low = (blocks - high.astype(F32)).astype(BF16)
    row = lax.broadcasted_iota(jnp.int32, (8, HALF), 0)
    picks = []
    for first in range(0, 64, 8):
        number = jnp.full((8, HALF), -1, jnp.int32)
        for slot in range(8):
            live = jnp.where(first + slot < cnt_ref[0, 0], ids_ref[0, first + slot], -1)
            number = jnp.where(row == slot, live, number)
        picks.append(jnp.where(number == lane, 1.0, 0.0))
    chosen = jnp.concatenate(picks, axis=0).astype(BF16)
    high = jnp.dot(chosen, high, preferred_element_type=F32).astype(BF16)
    low = jnp.dot(chosen, low, preferred_element_type=F32).astype(BF16)
    co_ref[...] = (
        jnp.dot(high, k_ref[0], preferred_element_type=F32)
        + jnp.dot(low, k_ref[0], preferred_element_type=F32)
        + jnp.dot(high, k_ref[1], preferred_element_type=F32)
    )


def on_device(volume, block_ids, counts):
    section = volume.reshape(COLS, ROWS)
    vmem = pl.BlockSpec(memory_space=pltpu.VMEM)
    smem = pl.BlockSpec(memory_space=pltpu.SMEM)
    hbm = pl.BlockSpec(memory_space=pl.ANY)
    stacked, basis = pl.pallas_call(
        exchange,
        out_shape=(
            jax.ShapeDtypeStruct((N_SEC, OUT_COLS, HALF), F32),
            jax.ShapeDtypeStruct((2, 512, 512), BF16),
        ),
        in_specs=[hbm],
        out_specs=(vmem, vmem),
        scratch_shapes=[
            pltpu.VMEM((2, COLS + 2 * PAD, HALF), F32),
            pltpu.VMEM((N_SEC, OUT_COLS, HALF), F32),
            pltpu.VMEM((2, 8, HALF), F32),
            pltpu.VMEM((2, 8, HALF), F32),
            pltpu.SemaphoreType.DMA((CHUNKS, 2)),
            pltpu.SemaphoreType.DMA,
            pltpu.SemaphoreType.DMA((N_SEC,)),
            pltpu.SemaphoreType.DMA((2,)),
            pltpu.SemaphoreType.DMA((2,)),
            pltpu.SemaphoreType.REGULAR,
            pltpu.SemaphoreType.DMA((GROUP_Z,)),
            pltpu.SemaphoreType.DMA((GROUP_Z,)),
        ],
        compiler_params=pltpu.CompilerParams(
            collective_id=0, has_side_effects=True, vmem_limit_bytes=207 * 256 * 1024
        ),
    )(section)
    downsampled, coeffs = pl.pallas_call(
        transform,
        out_shape=(
            jax.ShapeDtypeStruct((DEPTH, OUT_COLS, HALF), F32),
            jax.ShapeDtypeStruct((64, 512), F32),
        ),
        in_specs=[vmem, vmem, smem, smem],
        out_specs=(vmem, vmem),
        scratch_shapes=[pltpu.VMEM((4, HALF, HALF), F32)],
        compiler_params=pltpu.CompilerParams(vmem_limit_bytes=16 * 1024 * 1024),
    )(stacked, basis, block_ids.reshape(1, 64), counts)
    return downsampled, coeffs.reshape(1, 1, 64, 512)


def solution(mesh):
    placed = (P("sec", None, "yb"), P("sec", "yb", None), P("sec", "yb"))
    return jax.shard_map(
        on_device,
        mesh=mesh,
        in_specs=placed,
        out_specs=(P(None, "sec", "yb"), P("sec", "yb", None, None)),
        check_vma=False,
    )
```

```python
import functools
import math

import jax
import jax.numpy as jnp
from jax import lax
from jax.experimental import pallas as pl
from jax.experimental.pallas import tpu as pltpu
from jax.sharding import PartitionSpec as P

F32 = jnp.float32
BF16 = jnp.bfloat16
MESH = pl.DeviceIdType.MESH
NY, NZ = 4, 16
N_SEC = NY * NZ
N_YB = 8
COLS = 2048
ROWS = 256
HALF = 128
OUT_COLS = 16
DEPTH = 32
CHUNKS = 8
PAD = 8
GROUP_Z = NZ // 2
WINDOW = 2
OWN_ROUNDS = 4


def cosines(frequency, place):
    turn = ((2 * place + 1) * frequency) % 32
    value = jnp.zeros(turn.shape, F32)
    for step in range(32):
        value = jnp.where(turn == step, math.cos(math.pi * step / 16.0), value)
    return value * jnp.where(frequency == 0, math.sqrt(1.0 / 8.0), math.sqrt(2.0 / 8.0))


def fill_basis(k_ref):
    place = lax.broadcasted_iota(jnp.int32, (8, 512), 0)
    output = lax.broadcasted_iota(jnp.int32, (8, 512), 1)
    along_depth = cosines(output // 64, place)
    along_column = cosines(output // 8 % 8, place)
    along_row = cosines(output % 8, place)
    for c in range(8):
        for a in range(0, 8, 2):
            parts = [
                along_column * (along_row[c : c + 1, :] * along_depth[a + i : a + i + 1, :])
                for i in range(2)
            ]
            value = jnp.concatenate(parts, axis=0)
            high = value.astype(BF16)
            rows = pl.ds(64 * c + 8 * a, 16)
            k_ref[0, rows, :] = high
            k_ref[1, rows, :] = (value - high.astype(F32)).astype(BF16)


def row_matrix(half):
    inputs = lax.broadcasted_iota(jnp.int32, (HALF, HALF), 0) + half * HALF
    outputs = lax.broadcasted_iota(jnp.int32, (HALF, HALF), 1)
    offset = inputs - (2 * outputs - 1)
    weight = jnp.where((offset == 0) | (offset == 3), 0.125, 0.375)
    return jnp.where((offset >= 0) & (offset <= 3), weight, 0.0).astype(BF16)


def pieces(value):
    high = value.astype(BF16)
    rest = value - high.astype(F32)
    mid = rest.astype(BF16)
    return high, mid, (rest - mid.astype(F32)).astype(BF16)


def exchange(
    x_hbm, stacked, k_ref,
    xbuf, plane, edge_out, edge_in,
    x_sem, send_sem, recv_sem, edge_send, edge_recv, late_sem, up_sem, down_sem,
):
    me = lax.axis_index("sec")
    band = lax.axis_index("yb")
    y, z = me // NZ, me % NZ
    size = COLS // CHUNKS
    out_size = size // 2

    def load(chunk, half):
        return pltpu.make_async_copy(
            x_hbm.at[pl.ds(chunk * size, size), pl.ds(half * HALF, HALF)],
            xbuf.at[half, pl.ds(PAD + chunk * size, size), :],
            x_sem.at[chunk, half],
        )

    edge_in[...] = jnp.zeros(edge_in.shape, F32)
    for chunk in range(CHUNKS):
        for half in range(2):
            load(chunk, half).start()

    late = z >= GROUP_Z

    def signal(semaphore, column, row):
        pl.semaphore_signal(semaphore, inc=1, device_id=(column, row), device_id_type=MESH)

    def visit_group(visit, own):
        def step(index, carry):
            turn, dy = index // NY, index % NY
            hop = turn // 2
            dz = jnp.where(turn % 2 == 0, NZ // 2 - hop, hop - (NZ // 2 - 1))
            target = (z + dz + NZ) % NZ
            same = (target >= GROUP_Z) == late

            @pl.when(same if own else jnp.logical_not(same))
            def _():
                visit(((y + dy) % NY) * NZ + target)

            return carry

        lax.fori_loop(0, NY * (NZ - 1), step, 0)
        if own:
            for dy in range(1, NY):
                visit(((y + dy) % NY) * NZ + z)

    barrier = pltpu.get_barrier_semaphore()

    @pl.when(band > 0)
    def _():
        signal(barrier, me, band - 1)

    @pl.when(band < N_YB - 1)
    def _():
        signal(barrier, me, band + 1)

    @pl.when(jnp.logical_not(late))
    def _():
        visit_group(lambda column: signal(barrier, column, band), False)
        visit_group(lambda column: signal(barrier, column, band), True)

    for half in range(2):
        xbuf[half, pl.ds(0, PAD), :] = jnp.zeros((PAD, HALF), F32)
        xbuf[half, pl.ds(PAD + COLS, PAD), :] = jnp.zeros((PAD, HALF), F32)

    lane = lax.broadcasted_iota(jnp.int32, (8, HALF), 1)
    row_weights = [row_matrix(half) for half in range(2)]
    first_row = jnp.zeros((8, HALF), F32)
    last_row = jnp.zeros((8, HALF), F32)
    for half in range(2):
        load(0, half).wait()
    for chunk in range(CHUNKS):
        if chunk + 1 < CHUNKS:
            for half in range(2):
                load(chunk + 1, half).wait()
        total = jnp.zeros((out_size, HALF), F32)
        for half in range(2):
            start = PAD + chunk * size - 1
            taps = [xbuf[half, pl.ds(start + a, out_size, stride=2), :] for a in range(4)]
            narrow = (taps[0] + taps[3] + 3.0 * (taps[1] + taps[2])) * 0.125
            for part in pieces(narrow):
                total += jnp.dot(
                    part, row_weights[half], preferred_element_type=F32
                )
            for inner in range(out_size // 8):
                group = chunk * (out_size // 8) + inner
                rows = narrow[inner * 8 : inner * 8 + 8, :]
                if half == 0:
                    moved = rows if group == 0 else pltpu.roll(rows, group, 1)
                    first_row = jnp.where(lane == group, moved, first_row)
                else:
                    shift = (group + 1) % HALF
                    moved = rows if shift == 0 else pltpu.roll(rows, shift, 1)
                    last_row = jnp.where(lane == group, moved, last_row)
        per = out_size // OUT_COLS
        plane[pl.ds(chunk * per, per)] = total.reshape(per, OUT_COLS, HALF)
    edge_out[0] = first_row * 0.125
    edge_out[1] = last_row * 0.125

    inside = (band > 0).astype(jnp.int32) + (band < N_YB - 1).astype(jnp.int32)
    pl.semaphore_wait(barrier, NY * GROUP_Z - 1 + inside + late.astype(jnp.int32))

    def edge_copy(which, target):
        return pltpu.make_async_remote_copy(
            src_ref=edge_out.at[which],
            dst_ref=edge_in.at[which],
            send_sem=edge_send.at[which],
            recv_sem=edge_recv.at[which],
            device_id=(me, target),
            device_id_type=MESH,
        )

    @pl.when(band > 0)
    def _():
        edge_copy(0, band - 1).start()

    @pl.when(band < N_YB - 1)
    def _():
        edge_copy(1, band + 1).start()

    @pl.when(late)
    def _():
        visit_group(lambda column: signal(late_sem, column, band), False)

    @pl.when(band < N_YB - 1)
    def _():
        edge_copy(0, band + 1).wait_recv()

    @pl.when(band > 0)
    def _():
        edge_copy(1, band - 1).wait_recv()

    above, below = edge_in[0], edge_in[1]

    for group in range(COLS // 16):
        low = below if group == 0 else pltpu.roll(below, HALF - group, 1)
        high = above if group == HALF - 1 else pltpu.roll(above, HALF - 1 - group, 1)
        rows = pl.ds(group % 2 * 8, 8)
        plane[group // 2, rows, :] += jnp.where(lane == 0, low, 0.0) + jnp.where(
            lane == HALF - 1, high, 0.0
        )

    def chunk_copy(target, slot, semaphore=send_sem):
        return pltpu.make_async_remote_copy(
            src_ref=plane.at[target],
            dst_ref=stacked.at[slot],
            send_sem=semaphore,
            recv_sem=recv_sem.at[slot],
            device_id=(target, band),
            device_id_type=MESH,
        )

    def send(target):
        chunk_copy(target, me).start()

    stacked[me] = plane[me]

    def sent(semaphore, count):
        pltpu.make_async_remote_copy(
            src_ref=plane.at[pl.ds(0, count)],
            dst_ref=stacked.at[pl.ds(0, count)],
            send_sem=semaphore,
            recv_sem=recv_sem.at[0],
            device_id=((me + 1) % N_SEC, band),
            device_id_type=MESH,
        ).wait_send()

    place = z - GROUP_Z
    own_round = 1 + 2 * (band % 2)

    def sent_round(index):
        @pl.when(index < place)
        def _():
            sent(up_sem.at[index], NY)

        @pl.when(index + place < GROUP_Z)
        def _():
            sent(down_sem.at[index], NY)

    def send_round(index, carry):
        @pl.when(index >= WINDOW)
        def _():
            sent_round(index - WINDOW)

        for dy in range(NY):
            column = ((y + dy) % NY) * NZ

            @pl.when(index < place)
            def _():
                chunk_copy(column + index, me, up_sem.at[index]).start()

            @pl.when(index + place < GROUP_Z)
            def _():
                chunk_copy(column + place + index, me, down_sem.at[index]).start()

        @pl.when(index == own_round)
        def _():
            pl.semaphore_wait(late_sem, 1)

        @pl.when((index >= own_round) & (index < own_round + OWN_ROUNDS))
        def _():
            for half in range(GROUP_Z // OWN_ROUNDS):
                turn = (index - own_round) * (GROUP_Z // OWN_ROUNDS) + half
                target = GROUP_Z + (place + turn) % GROUP_Z

                @pl.when(turn > 0)
                def _():
                    send(y * NZ + target)

                for dy in range(1, NY):
                    send(((y + dy) % NY) * NZ + target)

        return carry

    @pl.when(late)
    def _():
        lax.fori_loop(0, GROUP_Z, send_round, 0)
        for index in range(GROUP_Z - WINDOW, GROUP_Z):
            sent_round(index)

    @pl.when(jnp.logical_not(late))
    def _():
        visit_group(send, True)
        pl.semaphore_wait(late_sem, NY * GROUP_Z)
        signal(late_sem, me + GROUP_Z, band)
        visit_group(send, False)

    fill_basis(k_ref)

    def receive(step, carry):
        origin = (me + step) % N_SEC
        chunk_copy(origin, origin).wait_recv()
        return carry

    lax.fori_loop(1, N_SEC, receive, 0)

    sent(send_sem, NY * GROUP_Z - 1)

    @pl.when(jnp.logical_not(late))
    def _():
        sent(send_sem, NY * GROUP_Z)

    @pl.when(band > 0)
    def _():
        edge_copy(0, band - 1).wait_send()

    @pl.when(band < N_YB - 1)
    def _():
        edge_copy(1, band + 1).wait_send()


def transform(stacked, k_ref, ids_ref, cnt_ref, ds_ref, co_ref, turned):
    for bz in range(DEPTH // 8):
        for k in range(8 * bz, 8 * bz + 8):
            value = 3.0 * (stacked[2 * k] + stacked[2 * k + 1])
            if k > 0:
                value += stacked[2 * k - 1]
            if k < DEPTH - 1:
                value += stacked[2 * k + 2]
            ds_ref[k] = value * 0.125
        group = ds_ref[pl.ds(8 * bz, 8)] - 0.5
        flat = jnp.concatenate(
            [group[:, 0:8, :].reshape(64, HALF), group[:, 8:16, :].reshape(64, HALF)], axis=0
        )
        turned[bz] = flat.T

    lane = lax.broadcasted_iota(jnp.int32, (8, HALF), 1)
    wide = lax.broadcasted_iota(jnp.int32, (16, HALF), 1)
    tiles = []
    for pair in range(4):
        rows = []
        for bz in range(DEPTH // 8):
            even = turned[bz, pl.ds(2 * pair, 16, stride=8), :]
            odd = turned[bz, pl.ds(2 * pair + 1, 16, stride=8), :]
            rows.append(jnp.where(wide < 64, even, pltpu.roll(odd, 64, 1)))
            rows.append(jnp.where(wide < 64, pltpu.roll(even, 64, 1), odd))
        tiles.append(jnp.concatenate(rows, axis=0))
    blocks = jnp.concatenate(tiles, axis=1)
    high = blocks.astype(BF16)
    low = (blocks - high.astype(F32)).astype(BF16)
    row = lax.broadcasted_iota(jnp.int32, (8, HALF), 0)
    picks = []
    for first in range(0, 64, 8):
        number = jnp.full((8, HALF), -1, jnp.int32)
        for slot in range(8):
            live = jnp.where(first + slot < cnt_ref[0, 0], ids_ref[0, first + slot], -1)
            number = jnp.where(row == slot, live, number)
        picks.append(jnp.where(number == lane, 1.0, 0.0))
    chosen = jnp.concatenate(picks, axis=0).astype(BF16)
    high = jnp.dot(chosen, high, preferred_element_type=F32).astype(BF16)
    low = jnp.dot(chosen, low, preferred_element_type=F32).astype(BF16)
    both = jnp.dot(
        jnp.concatenate([high, low], axis=0), k_ref[0], preferred_element_type=F32
    )
    co_ref[...] = both[0:64] + both[64:128] + jnp.dot(
        high, k_ref[1], preferred_element_type=F32
    )


def on_device(volume, block_ids, counts):
    section = volume.reshape(COLS, ROWS)
    vmem = pl.BlockSpec(memory_space=pltpu.VMEM)
    smem = pl.BlockSpec(memory_space=pltpu.SMEM)
    hbm = pl.BlockSpec(memory_space=pl.ANY)
    stacked, basis = pl.pallas_call(
        exchange,
        out_shape=(
            jax.ShapeDtypeStruct((N_SEC, OUT_COLS, HALF), F32),
            jax.ShapeDtypeStruct((2, 512, 512), BF16),
        ),
        in_specs=[hbm],
        out_specs=(vmem, vmem),
        scratch_shapes=[
            pltpu.VMEM((2, COLS + 2 * PAD, HALF), F32),
            pltpu.VMEM((N_SEC, OUT_COLS, HALF), F32),
            pltpu.VMEM((2, 8, HALF), F32),
            pltpu.VMEM((2, 8, HALF), F32),
            pltpu.SemaphoreType.DMA((CHUNKS, 2)),
            pltpu.SemaphoreType.DMA,
            pltpu.SemaphoreType.DMA((N_SEC,)),
            pltpu.SemaphoreType.DMA((2,)),
            pltpu.SemaphoreType.DMA((2,)),
            pltpu.SemaphoreType.REGULAR,
            pltpu.SemaphoreType.DMA((GROUP_Z,)),
            pltpu.SemaphoreType.DMA((GROUP_Z,)),
        ],
        compiler_params=pltpu.CompilerParams(
            collective_id=0, has_side_effects=True, vmem_limit_bytes=207 * 256 * 1024
        ),
    )(section)
    downsampled, coeffs = pl.pallas_call(
        transform,
        out_shape=(
            jax.ShapeDtypeStruct((DEPTH, OUT_COLS, HALF), F32),
            jax.ShapeDtypeStruct((64, 512), F32),
        ),
        in_specs=[vmem, vmem, smem, smem],
        out_specs=(vmem, vmem),
        scratch_shapes=[pltpu.VMEM((4, HALF, HALF), F32)],
        compiler_params=pltpu.CompilerParams(vmem_limit_bytes=16 * 1024 * 1024),
    )(stacked, basis, block_ids.reshape(1, 64), counts)
    return downsampled, coeffs.reshape(1, 1, 64, 512)


def solution(mesh):
    placed = (P("sec", None, "yb"), P("sec", "yb", None), P("sec", "yb"))
    return jax.shard_map(
        on_device,
        mesh=mesh,
        in_specs=placed,
        out_specs=(P(None, "sec", "yb"), P("sec", "yb", None, None)),
        check_vma=False,
    )
```

```python
import functools
import math

import jax
import jax.numpy as jnp
from jax import lax
from jax.experimental import pallas as pl
from jax.experimental.pallas import tpu as pltpu
from jax.sharding import PartitionSpec as P

F32 = jnp.float32
BF16 = jnp.bfloat16
MESH = pl.DeviceIdType.MESH
NY, NZ = 4, 16
N_SEC = NY * NZ
N_YB = 8
COLS = 2048
ROWS = 256
HALF = 128
OUT_COLS = 16
DEPTH = 32
CHUNKS = 8
PAD = 8
GROUP_Z = NZ // 2
WINDOW = 2
OWN_ROUNDS = 4


def cosines(frequency, place):
    turn = ((2 * place + 1) * frequency) % 32
    value = jnp.zeros(turn.shape, F32)
    for step in range(32):
        value = jnp.where(turn == step, math.cos(math.pi * step / 16.0), value)
    return value * jnp.where(frequency == 0, math.sqrt(1.0 / 8.0), math.sqrt(2.0 / 8.0))


def fill_basis(k_ref):
    place = lax.broadcasted_iota(jnp.int32, (8, 512), 0)
    output = lax.broadcasted_iota(jnp.int32, (8, 512), 1)
    along_depth = cosines(output // 64, place)
    along_column = cosines(output // 8 % 8, place)
    along_row = cosines(output % 8, place)
    for c in range(8):
        for a in range(0, 8, 2):
            parts = [
                along_column * (along_row[c : c + 1, :] * along_depth[a + i : a + i + 1, :])
                for i in range(2)
            ]
            value = jnp.concatenate(parts, axis=0)
            high = value.astype(BF16)
            rows = pl.ds(64 * c + 8 * a, 16)
            k_ref[0, rows, :] = high
            k_ref[1, rows, :] = (value - high.astype(F32)).astype(BF16)


def row_matrix(half):
    inputs = lax.broadcasted_iota(jnp.int32, (HALF, HALF), 0) + half * HALF
    outputs = lax.broadcasted_iota(jnp.int32, (HALF, HALF), 1)
    offset = inputs - (2 * outputs - 1)
    weight = jnp.where((offset == 0) | (offset == 3), 0.125, 0.375)
    return jnp.where((offset >= 0) & (offset <= 3), weight, 0.0).astype(BF16)


def pieces(value):
    high = value.astype(BF16)
    rest = value - high.astype(F32)
    mid = rest.astype(BF16)
    return high, mid, (rest - mid.astype(F32)).astype(BF16)


def exchange(
    x_hbm, stacked, k_ref,
    xbuf, plane, edge_out, edge_in,
    x_sem, send_sem, recv_sem, edge_send, edge_recv, late_sem, up_sem, down_sem,
):
    me = lax.axis_index("sec")
    band = lax.axis_index("yb")
    y, z = me // NZ, me % NZ
    size = COLS // CHUNKS
    out_size = size // 2

    def load(chunk, half):
        return pltpu.make_async_copy(
            x_hbm.at[pl.ds(chunk * size, size), pl.ds(half * HALF, HALF)],
            xbuf.at[half, pl.ds(PAD + chunk * size, size), :],
            x_sem.at[chunk, half],
        )

    edge_in[...] = jnp.zeros(edge_in.shape, F32)
    for chunk in range(CHUNKS):
        for half in range(2):
            load(chunk, half).start()

    late = z >= GROUP_Z

    def signal(semaphore, column, row):
        pl.semaphore_signal(semaphore, inc=1, device_id=(column, row), device_id_type=MESH)

    def visit_group(visit, own):
        def step(index, carry):
            turn, dy = index // NY, index % NY
            hop = turn // 2
            dz = jnp.where(turn % 2 == 0, NZ // 2 - hop, hop - (NZ // 2 - 1))
            target = (z + dz + NZ) % NZ
            same = (target >= GROUP_Z) == late

            @pl.when(same if own else jnp.logical_not(same))
            def _():
                visit(((y + dy) % NY) * NZ + target)

            return carry

        lax.fori_loop(0, NY * (NZ - 1), step, 0)
        if own:
            for dy in range(1, NY):
                visit(((y + dy) % NY) * NZ + z)

    barrier = pltpu.get_barrier_semaphore()

    @pl.when(band > 0)
    def _():
        signal(barrier, me, band - 1)

    @pl.when(band < N_YB - 1)
    def _():
        signal(barrier, me, band + 1)

    @pl.when(jnp.logical_not(late))
    def _():
        visit_group(lambda column: signal(barrier, column, band), False)
        visit_group(lambda column: signal(barrier, column, band), True)

    for half in range(2):
        xbuf[half, pl.ds(0, PAD), :] = jnp.zeros((PAD, HALF), F32)
        xbuf[half, pl.ds(PAD + COLS, PAD), :] = jnp.zeros((PAD, HALF), F32)

    lane = lax.broadcasted_iota(jnp.int32, (8, HALF), 1)
    row_weights = [row_matrix(half) for half in range(2)]
    first_row = jnp.zeros((8, HALF), F32)
    last_row = jnp.zeros((8, HALF), F32)
    for half in range(2):
        load(0, half).wait()
    for chunk in range(CHUNKS):
        if chunk + 1 < CHUNKS:
            for half in range(2):
                load(chunk + 1, half).wait()
        total = jnp.zeros((out_size, HALF), F32)
        for half in range(2):
            start = PAD + chunk * size - 1
            taps = [xbuf[half, pl.ds(start + a, out_size, stride=2), :] for a in range(4)]
            narrow = (taps[0] + taps[3] + 3.0 * (taps[1] + taps[2])) * 0.125
            for part in pieces(narrow):
                total += jnp.dot(
                    part, row_weights[half], preferred_element_type=F32
                )
            for inner in range(out_size // 8):
                group = chunk * (out_size // 8) + inner
                rows = narrow[inner * 8 : inner * 8 + 8, :]
                if half == 0:
                    moved = rows if group == 0 else pltpu.roll(rows, group, 1)
                    first_row = jnp.where(lane == group, moved, first_row)
                else:
                    shift = (group + 1) % HALF
                    moved = rows if shift == 0 else pltpu.roll(rows, shift, 1)
                    last_row = jnp.where(lane == group, moved, last_row)
        per = out_size // OUT_COLS
        plane[pl.ds(chunk * per, per)] = total.reshape(per, OUT_COLS, HALF)
    edge_out[0] = first_row * 0.125
    edge_out[1] = last_row * 0.125

    inside = (band > 0).astype(jnp.int32) + (band < N_YB - 1).astype(jnp.int32)
    pl.semaphore_wait(barrier, NY * GROUP_Z - 1 + inside + late.astype(jnp.int32))

    def edge_copy(which, target):
        return pltpu.make_async_remote_copy(
            src_ref=edge_out.at[which],
            dst_ref=edge_in.at[which],
            send_sem=edge_send.at[which],
            recv_sem=edge_recv.at[which],
            device_id=(me, target),
            device_id_type=MESH,
        )

    @pl.when(band > 0)
    def _():
        edge_copy(0, band - 1).start()

    @pl.when(band < N_YB - 1)
    def _():
        edge_copy(1, band + 1).start()

    @pl.when(late)
    def _():
        visit_group(lambda column: signal(late_sem, column, band), False)

    @pl.when(band < N_YB - 1)
    def _():
        edge_copy(0, band + 1).wait_recv()

    @pl.when(band > 0)
    def _():
        edge_copy(1, band - 1).wait_recv()

    above, below = edge_in[0], edge_in[1]

    for group in range(COLS // 16):
        low = below if group == 0 else pltpu.roll(below, HALF - group, 1)
        high = above if group == HALF - 1 else pltpu.roll(above, HALF - 1 - group, 1)
        rows = pl.ds(group % 2 * 8, 8)
        plane[group // 2, rows, :] += jnp.where(lane == 0, low, 0.0) + jnp.where(
            lane == HALF - 1, high, 0.0
        )

    def chunk_copy(target, slot, semaphore=send_sem):
        return pltpu.make_async_remote_copy(
            src_ref=plane.at[target],
            dst_ref=stacked.at[slot],
            send_sem=semaphore,
            recv_sem=recv_sem,
            device_id=(target, band),
            device_id_type=MESH,
        )

    def send(target):
        chunk_copy(target, me).start()

    stacked[me] = plane[me]

    def sent(semaphore, count):
        pltpu.make_async_remote_copy(
            src_ref=plane.at[pl.ds(0, count)],
            dst_ref=stacked.at[pl.ds(0, count)],
            send_sem=semaphore,
            recv_sem=recv_sem,
            device_id=((me + 1) % N_SEC, band),
            device_id_type=MESH,
        ).wait_send()

    place = z - GROUP_Z
    own_round = 1 + 2 * (band % 2)

    def sent_round(index):
        @pl.when(index < place)
        def _():
            sent(up_sem.at[index], NY)

        @pl.when(index + place < GROUP_Z)
        def _():
            sent(down_sem.at[index], NY)

    def send_round(index, carry):
        @pl.when(index >= WINDOW)
        def _():
            sent_round(index - WINDOW)

        for dy in range(NY):
            column = ((y + dy) % NY) * NZ

            @pl.when(index < place)
            def _():
                chunk_copy(column + index, me, up_sem.at[index]).start()

            @pl.when(index + place < GROUP_Z)
            def _():
                chunk_copy(column + place + index, me, down_sem.at[index]).start()

        @pl.when(index == own_round)
        def _():
            pl.semaphore_wait(late_sem, 1)

        @pl.when((index >= own_round) & (index < own_round + OWN_ROUNDS))
        def _():
            for half in range(GROUP_Z // OWN_ROUNDS):
                turn = (index - own_round) * (GROUP_Z // OWN_ROUNDS) + half
                target = GROUP_Z + (place + turn) % GROUP_Z

                @pl.when(turn > 0)
                def _():
                    send(y * NZ + target)

                for dy in range(1, NY):
                    send(((y + dy) % NY) * NZ + target)

        return carry

    @pl.when(late)
    def _():
        lax.fori_loop(0, GROUP_Z, send_round, 0)
        for index in range(GROUP_Z - WINDOW, GROUP_Z):
            sent_round(index)

    @pl.when(jnp.logical_not(late))
    def _():
        visit_group(send, True)
        pl.semaphore_wait(late_sem, NY * GROUP_Z)
        signal(late_sem, me + GROUP_Z, band)
        visit_group(send, False)

    fill_basis(k_ref)

    pltpu.make_async_remote_copy(
        src_ref=plane.at[pl.ds(0, N_SEC - 1)],
        dst_ref=stacked.at[pl.ds(0, N_SEC - 1)],
        send_sem=send_sem,
        recv_sem=recv_sem,
        device_id=((me + 1) % N_SEC, band),
        device_id_type=MESH,
    ).wait_recv()

    sent(send_sem, NY * GROUP_Z - 1)

    @pl.when(jnp.logical_not(late))
    def _():
        sent(send_sem, NY * GROUP_Z)

    @pl.when(band > 0)
    def _():
        edge_copy(0, band - 1).wait_send()

    @pl.when(band < N_YB - 1)
    def _():
        edge_copy(1, band + 1).wait_send()


def transform(stacked, k_ref, ids_ref, cnt_ref, ds_ref, co_ref, turned):
    for bz in range(DEPTH // 8):
        for k in range(8 * bz, 8 * bz + 8):
            value = 3.0 * (stacked[2 * k] + stacked[2 * k + 1])
            if k > 0:
                value += stacked[2 * k - 1]
            if k < DEPTH - 1:
                value += stacked[2 * k + 2]
            ds_ref[k] = value * 0.125
        group = ds_ref[pl.ds(8 * bz, 8)] - 0.5
        flat = jnp.concatenate(
            [group[:, 0:8, :].reshape(64, HALF), group[:, 8:16, :].reshape(64, HALF)], axis=0
        )
        turned[bz] = flat.T

    lane = lax.broadcasted_iota(jnp.int32, (8, HALF), 1)
    wide = lax.broadcasted_iota(jnp.int32, (16, HALF), 1)
    tiles = []
    for pair in range(4):
        rows = []
        for bz in range(DEPTH // 8):
            even = turned[bz, pl.ds(2 * pair, 16, stride=8), :]
            odd = turned[bz, pl.ds(2 * pair + 1, 16, stride=8), :]
            rows.append(jnp.where(wide < 64, even, pltpu.roll(odd, 64, 1)))
            rows.append(jnp.where(wide < 64, pltpu.roll(even, 64, 1), odd))
        tiles.append(jnp.concatenate(rows, axis=0))
    blocks = jnp.concatenate(tiles, axis=1)
    high = blocks.astype(BF16)
    low = (blocks - high.astype(F32)).astype(BF16)
    row = lax.broadcasted_iota(jnp.int32, (8, HALF), 0)
    picks = []
    for first in range(0, 64, 8):
        number = jnp.full((8, HALF), -1, jnp.int32)
        for slot in range(8):
            live = jnp.where(first + slot < cnt_ref[0, 0], ids_ref[0, first + slot], -1)
            number = jnp.where(row == slot, live, number)
        picks.append(jnp.where(number == lane, 1.0, 0.0))
    chosen = jnp.concatenate(picks, axis=0).astype(BF16)
    high = jnp.dot(chosen, high, preferred_element_type=F32).astype(BF16)
    low = jnp.dot(chosen, low, preferred_element_type=F32).astype(BF16)
    both = jnp.dot(
        jnp.concatenate([high, low], axis=0), k_ref[0], preferred_element_type=F32
    )
    co_ref[...] = both[0:64] + both[64:128] + jnp.dot(
        high, k_ref[1], preferred_element_type=F32
    )


def on_device(volume, block_ids, counts):
    section = volume.reshape(COLS, ROWS)
    vmem = pl.BlockSpec(memory_space=pltpu.VMEM)
    smem = pl.BlockSpec(memory_space=pltpu.SMEM)
    hbm = pl.BlockSpec(memory_space=pl.ANY)
    stacked, basis = pl.pallas_call(
        exchange,
        out_shape=(
            jax.ShapeDtypeStruct((N_SEC, OUT_COLS, HALF), F32),
            jax.ShapeDtypeStruct((2, 512, 512), BF16),
        ),
        in_specs=[hbm],
        out_specs=(vmem, vmem),
        scratch_shapes=[
            pltpu.VMEM((2, COLS + 2 * PAD, HALF), F32),
            pltpu.VMEM((N_SEC, OUT_COLS, HALF), F32),
            pltpu.VMEM((2, 8, HALF), F32),
            pltpu.VMEM((2, 8, HALF), F32),
            pltpu.SemaphoreType.DMA((CHUNKS, 2)),
            pltpu.SemaphoreType.DMA,
            pltpu.SemaphoreType.DMA,
            pltpu.SemaphoreType.DMA((2,)),
            pltpu.SemaphoreType.DMA((2,)),
            pltpu.SemaphoreType.REGULAR,
            pltpu.SemaphoreType.DMA((GROUP_Z,)),
            pltpu.SemaphoreType.DMA((GROUP_Z,)),
        ],
        compiler_params=pltpu.CompilerParams(
            collective_id=0, has_side_effects=True, vmem_limit_bytes=207 * 256 * 1024
        ),
    )(section)
    downsampled, coeffs = pl.pallas_call(
        transform,
        out_shape=(
            jax.ShapeDtypeStruct((DEPTH, OUT_COLS, HALF), F32),
            jax.ShapeDtypeStruct((64, 512), F32),
        ),
        in_specs=[vmem, vmem, smem, smem],
        out_specs=(vmem, vmem),
        scratch_shapes=[pltpu.VMEM((4, HALF, HALF), F32)],
        compiler_params=pltpu.CompilerParams(vmem_limit_bytes=16 * 1024 * 1024),
    )(stacked, basis, block_ids.reshape(1, 64), counts)
    return downsampled, coeffs.reshape(1, 1, 64, 512)


def solution(mesh):
    placed = (P("sec", None, "yb"), P("sec", "yb", None), P("sec", "yb"))
    return jax.shard_map(
        on_device,
        mesh=mesh,
        in_specs=placed,
        out_specs=(P(None, "sec", "yb"), P("sec", "yb", None, None)),
        check_vma=False,
    )
```

```python
import functools
import math

import jax
import jax.numpy as jnp
from jax import lax
from jax.experimental import pallas as pl
from jax.experimental.pallas import tpu as pltpu
from jax.sharding import PartitionSpec as P

F32 = jnp.float32
BF16 = jnp.bfloat16
MESH = pl.DeviceIdType.MESH
NY, NZ = 4, 16
N_SEC = NY * NZ
N_YB = 8
COLS = 2048
ROWS = 256
HALF = 128
OUT_COLS = 16
DEPTH = 32
CHUNKS = 8
PAD = 8
GROUP_Z = NZ // 2
WINDOW = 2
OWN_ROUNDS = 4


def cosines(frequency, place):
    turn = ((2 * place + 1) * frequency) % 32
    value = jnp.zeros(turn.shape, F32)
    for step in range(32):
        value = jnp.where(turn == step, math.cos(math.pi * step / 16.0), value)
    return value * jnp.where(frequency == 0, math.sqrt(1.0 / 8.0), math.sqrt(2.0 / 8.0))


def fill_basis(k_ref):
    place = lax.broadcasted_iota(jnp.int32, (8, 512), 0)
    output = lax.broadcasted_iota(jnp.int32, (8, 512), 1)
    along_depth = cosines(output // 64, place)
    along_column = cosines(output // 8 % 8, place)
    along_row = cosines(output % 8, place)
    for c in range(8):
        for a in range(0, 8, 2):
            parts = [
                along_column * (along_row[c : c + 1, :] * along_depth[a + i : a + i + 1, :])
                for i in range(2)
            ]
            value = jnp.concatenate(parts, axis=0)
            high = value.astype(BF16)
            rows = pl.ds(64 * c + 8 * a, 16)
            k_ref[0, rows, :] = high
            k_ref[1, rows, :] = (value - high.astype(F32)).astype(BF16)


def row_matrix(half):
    inputs = lax.broadcasted_iota(jnp.int32, (HALF, HALF), 0) + half * HALF
    outputs = lax.broadcasted_iota(jnp.int32, (HALF, HALF), 1)
    offset = inputs - (2 * outputs - 1)
    weight = jnp.where((offset == 0) | (offset == 3), 0.125, 0.375)
    return jnp.where((offset >= 0) & (offset <= 3), weight, 0.0).astype(BF16)


def pieces(value):
    high = value.astype(BF16)
    rest = value - high.astype(F32)
    mid = rest.astype(BF16)
    return high, mid, (rest - mid.astype(F32)).astype(BF16)


def exchange(
    x_hbm, stacked, k_ref,
    xbuf, plane, edge_out, edge_in,
    x_sem, send_sem, recv_sem, edge_send, edge_recv, late_sem, up_sem, down_sem,
):
    me = lax.axis_index("sec")
    band = lax.axis_index("yb")
    y, z = me // NZ, me % NZ
    size = COLS // CHUNKS
    out_size = size // 2

    def load(chunk, half):
        return pltpu.make_async_copy(
            x_hbm.at[pl.ds(chunk * size, size), pl.ds(half * HALF, HALF)],
            xbuf.at[half, pl.ds(PAD + chunk * size, size), :],
            x_sem.at[chunk, half],
        )

    edge_in[...] = jnp.zeros(edge_in.shape, F32)
    for chunk in range(CHUNKS):
        for half in range(2):
            load(chunk, half).start()

    late = z >= GROUP_Z

    def signal(semaphore, column, row):
        pl.semaphore_signal(semaphore, inc=1, device_id=(column, row), device_id_type=MESH)

    def visit_group(visit, own):
        def step(index, carry):
            turn, dy = index // NY, index % NY
            hop = turn // 2
            dz = jnp.where(turn % 2 == 0, NZ // 2 - hop, hop - (NZ // 2 - 1))
            target = (z + dz + NZ) % NZ
            same = (target >= GROUP_Z) == late

            @pl.when(same if own else jnp.logical_not(same))
            def _():
                visit(((y + dy) % NY) * NZ + target)

            return carry

        lax.fori_loop(0, NY * (NZ - 1), step, 0)
        if own:
            for dy in range(1, NY):
                visit(((y + dy) % NY) * NZ + z)

    barrier = pltpu.get_barrier_semaphore()

    @pl.when(band > 0)
    def _():
        signal(barrier, me, band - 1)

    @pl.when(band < N_YB - 1)
    def _():
        signal(barrier, me, band + 1)

    @pl.when(jnp.logical_not(late))
    def _():
        visit_group(lambda column: signal(barrier, column, band), False)
        visit_group(lambda column: signal(barrier, column, band), True)

    for half in range(2):
        xbuf[half, pl.ds(0, PAD), :] = jnp.zeros((PAD, HALF), F32)
        xbuf[half, pl.ds(PAD + COLS, PAD), :] = jnp.zeros((PAD, HALF), F32)

    lane = lax.broadcasted_iota(jnp.int32, (8, HALF), 1)
    row_weights = [row_matrix(half) for half in range(2)]
    first_row = jnp.zeros((8, HALF), F32)
    last_row = jnp.zeros((8, HALF), F32)
    for half in range(2):
        load(0, half).wait()
    for chunk in range(CHUNKS):
        if chunk + 1 < CHUNKS:
            for half in range(2):
                load(chunk + 1, half).wait()
        total = jnp.zeros((out_size, HALF), F32)
        for half in range(2):
            start = PAD + chunk * size - 1
            taps = [xbuf[half, pl.ds(start + a, out_size, stride=2), :] for a in range(4)]
            narrow = (taps[0] + taps[3] + 3.0 * (taps[1] + taps[2])) * 0.125
            for part in pieces(narrow):
                total += jnp.dot(
                    part, row_weights[half], preferred_element_type=F32
                )
            for inner in range(out_size // 8):
                group = chunk * (out_size // 8) + inner
                rows = narrow[inner * 8 : inner * 8 + 8, :]
                if half == 0:
                    moved = rows if group == 0 else pltpu.roll(rows, group, 1)
                    first_row = jnp.where(lane == group, moved, first_row)
                else:
                    shift = (group + 1) % HALF
                    moved = rows if shift == 0 else pltpu.roll(rows, shift, 1)
                    last_row = jnp.where(lane == group, moved, last_row)
        per = out_size // OUT_COLS
        plane[pl.ds(chunk * per, per)] = total.reshape(per, OUT_COLS, HALF)
    edge_out[0] = first_row * 0.125
    edge_out[1] = last_row * 0.125

    inside = (band > 0).astype(jnp.int32) + (band < N_YB - 1).astype(jnp.int32)
    pl.semaphore_wait(barrier, NY * GROUP_Z - 1 + inside + late.astype(jnp.int32))

    def edge_copy(which, target):
        return pltpu.make_async_remote_copy(
            src_ref=edge_out.at[which],
            dst_ref=edge_in.at[which],
            send_sem=edge_send.at[which],
            recv_sem=edge_recv.at[which],
            device_id=(me, target),
            device_id_type=MESH,
        )

    @pl.when(band > 0)
    def _():
        edge_copy(0, band - 1).start()

    @pl.when(band < N_YB - 1)
    def _():
        edge_copy(1, band + 1).start()

    @pl.when(late)
    def _():
        visit_group(lambda column: signal(late_sem, column, band), False)

    @pl.when(band < N_YB - 1)
    def _():
        edge_copy(0, band + 1).wait_recv()

    @pl.when(band > 0)
    def _():
        edge_copy(1, band - 1).wait_recv()

    above, below = edge_in[0], edge_in[1]

    for group in range(COLS // 16):
        low = below if group == 0 else pltpu.roll(below, HALF - group, 1)
        high = above if group == HALF - 1 else pltpu.roll(above, HALF - 1 - group, 1)
        rows = pl.ds(group % 2 * 8, 8)
        plane[group // 2, rows, :] += jnp.where(lane == 0, low, 0.0) + jnp.where(
            lane == HALF - 1, high, 0.0
        )

    def chunk_copy(target, slot, semaphore=send_sem):
        return pltpu.make_async_remote_copy(
            src_ref=plane.at[target],
            dst_ref=stacked.at[slot],
            send_sem=semaphore,
            recv_sem=recv_sem,
            device_id=(target, band),
            device_id_type=MESH,
        )

    def send(target):
        chunk_copy(target, me).start()

    stacked[me] = plane[me]

    def sent(semaphore, count):
        pltpu.make_async_remote_copy(
            src_ref=plane.at[pl.ds(0, count)],
            dst_ref=stacked.at[pl.ds(0, count)],
            send_sem=semaphore,
            recv_sem=recv_sem,
            device_id=((me + 1) % N_SEC, band),
            device_id_type=MESH,
        ).wait_send()

    place = z - GROUP_Z
    own_round = 1 + 2 * (band % 2)

    def sent_round(index):
        @pl.when(index < place)
        def _():
            sent(up_sem.at[index], NY)

        @pl.when(index + place < GROUP_Z)
        def _():
            sent(down_sem.at[index], NY)

    def send_round(index, carry):
        @pl.when(index >= WINDOW)
        def _():
            sent_round(index - WINDOW)

        for dy in range(NY):
            column = ((y + dy) % NY) * NZ

            @pl.when(index < place)
            def _():
                chunk_copy(column + index, me, up_sem.at[index]).start()

            @pl.when(index + place < GROUP_Z)
            def _():
                chunk_copy(column + place + index, me, down_sem.at[index]).start()

        @pl.when(index == own_round)
        def _():
            pl.semaphore_wait(late_sem, 1)

        @pl.when((index >= own_round) & (index < own_round + OWN_ROUNDS))
        def _():
            for half in range(GROUP_Z // OWN_ROUNDS):
                turn = (index - own_round) * (GROUP_Z // OWN_ROUNDS) + half
                target = GROUP_Z + (place + turn) % GROUP_Z

                @pl.when(turn > 0)
                def _():
                    send(y * NZ + target)

                for dy in range(1, NY):
                    send(((y + dy) % NY) * NZ + target)

        return carry

    @pl.when(late)
    def _():
        lax.fori_loop(0, GROUP_Z, send_round, 0)
        for index in range(GROUP_Z - WINDOW, GROUP_Z):
            sent_round(index)

    @pl.when(jnp.logical_not(late))
    def _():
        visit_group(send, True)
        pl.semaphore_wait(late_sem, NY * GROUP_Z)
        signal(late_sem, me + GROUP_Z, band)
        visit_group(send, False)

    fill_basis(k_ref)

    sent(send_sem, NY * GROUP_Z - 1)

    @pl.when(jnp.logical_not(late))
    def _():
        sent(send_sem, NY * GROUP_Z)

    @pl.when(band > 0)
    def _():
        edge_copy(0, band - 1).wait_send()

    @pl.when(band < N_YB - 1)
    def _():
        edge_copy(1, band + 1).wait_send()

    pltpu.make_async_remote_copy(
        src_ref=plane.at[pl.ds(0, N_SEC - 1)],
        dst_ref=stacked.at[pl.ds(0, N_SEC - 1)],
        send_sem=send_sem,
        recv_sem=recv_sem,
        device_id=((me + 1) % N_SEC, band),
        device_id_type=MESH,
    ).wait_recv()


def transform(stacked, k_ref, ids_ref, cnt_ref, ds_ref, co_ref, turned):
    for bz in range(DEPTH // 8):
        for k in range(8 * bz, 8 * bz + 8):
            value = 3.0 * (stacked[2 * k] + stacked[2 * k + 1])
            if k > 0:
                value += stacked[2 * k - 1]
            if k < DEPTH - 1:
                value += stacked[2 * k + 2]
            ds_ref[k] = value * 0.125
        group = ds_ref[pl.ds(8 * bz, 8)] - 0.5
        flat = jnp.concatenate(
            [group[:, 0:8, :].reshape(64, HALF), group[:, 8:16, :].reshape(64, HALF)], axis=0
        )
        turned[bz] = flat.T

    lane = lax.broadcasted_iota(jnp.int32, (8, HALF), 1)
    wide = lax.broadcasted_iota(jnp.int32, (16, HALF), 1)
    tiles = []
    for pair in range(4):
        rows = []
        for bz in range(DEPTH // 8):
            even = turned[bz, pl.ds(2 * pair, 16, stride=8), :]
            odd = turned[bz, pl.ds(2 * pair + 1, 16, stride=8), :]
            rows.append(jnp.where(wide < 64, even, pltpu.roll(odd, 64, 1)))
            rows.append(jnp.where(wide < 64, pltpu.roll(even, 64, 1), odd))
        tiles.append(jnp.concatenate(rows, axis=0))
    blocks = jnp.concatenate(tiles, axis=1)
    high = blocks.astype(BF16)
    low = (blocks - high.astype(F32)).astype(BF16)
    row = lax.broadcasted_iota(jnp.int32, (8, HALF), 0)
    picks = []
    for first in range(0, 64, 8):
        number = jnp.full((8, HALF), -1, jnp.int32)
        for slot in range(8):
            live = jnp.where(first + slot < cnt_ref[0, 0], ids_ref[0, first + slot], -1)
            number = jnp.where(row == slot, live, number)
        picks.append(jnp.where(number == lane, 1.0, 0.0))
    chosen = jnp.concatenate(picks, axis=0).astype(BF16)
    high = jnp.dot(chosen, high, preferred_element_type=F32).astype(BF16)
    low = jnp.dot(chosen, low, preferred_element_type=F32).astype(BF16)
    both = jnp.dot(
        jnp.concatenate([high, low], axis=0), k_ref[0], preferred_element_type=F32
    )
    co_ref[...] = both[0:64] + both[64:128] + jnp.dot(
        high, k_ref[1], preferred_element_type=F32
    )


def on_device(volume, block_ids, counts):
    section = volume.reshape(COLS, ROWS)
    vmem = pl.BlockSpec(memory_space=pltpu.VMEM)
    smem = pl.BlockSpec(memory_space=pltpu.SMEM)
    hbm = pl.BlockSpec(memory_space=pl.ANY)
    stacked, basis = pl.pallas_call(
        exchange,
        out_shape=(
            jax.ShapeDtypeStruct((N_SEC, OUT_COLS, HALF), F32),
            jax.ShapeDtypeStruct((2, 512, 512), BF16),
        ),
        in_specs=[hbm],
        out_specs=(vmem, vmem),
        scratch_shapes=[
            pltpu.VMEM((2, COLS + 2 * PAD, HALF), F32),
            pltpu.VMEM((N_SEC, OUT_COLS, HALF), F32),
            pltpu.VMEM((2, 8, HALF), F32),
            pltpu.VMEM((2, 8, HALF), F32),
            pltpu.SemaphoreType.DMA((CHUNKS, 2)),
            pltpu.SemaphoreType.DMA,
            pltpu.SemaphoreType.DMA,
            pltpu.SemaphoreType.DMA((2,)),
            pltpu.SemaphoreType.DMA((2,)),
            pltpu.SemaphoreType.REGULAR,
            pltpu.SemaphoreType.DMA((GROUP_Z,)),
            pltpu.SemaphoreType.DMA((GROUP_Z,)),
        ],
        compiler_params=pltpu.CompilerParams(
            collective_id=0, has_side_effects=True, vmem_limit_bytes=207 * 256 * 1024
        ),
    )(section)
    downsampled, coeffs = pl.pallas_call(
        transform,
        out_shape=(
            jax.ShapeDtypeStruct((DEPTH, OUT_COLS, HALF), F32),
            jax.ShapeDtypeStruct((64, 512), F32),
        ),
        in_specs=[vmem, vmem, smem, smem],
        out_specs=(vmem, vmem),
        scratch_shapes=[pltpu.VMEM((4, HALF, HALF), F32)],
        compiler_params=pltpu.CompilerParams(vmem_limit_bytes=16 * 1024 * 1024),
    )(stacked, basis, block_ids.reshape(1, 64), counts)
    return downsampled, coeffs.reshape(1, 1, 64, 512)


def solution(mesh):
    placed = (P("sec", None, "yb"), P("sec", "yb", None), P("sec", "yb"))
    return jax.shard_map(
        on_device,
        mesh=mesh,
        in_specs=placed,
        out_specs=(P(None, "sec", "yb"), P("sec", "yb", None, None)),
        check_vma=False,
    )
```
